512 devices in a mesh: req: 16 (over y, z_hi), head: 32 (over z_lo, x, core).
Axes of the slice: x: 4, y: 4, z: 16 (z_hi: 4, z_lo: 4; z = z_hi * 4 + z_lo), core: 2. Of those that a mesh axis runs over, the one named last changes fastest.
Arguments:
- queries: bfloat16 [6144, 128, 192], P('req', 'head'), may hold values from -128 to 128
- d_out: bfloat16 [6144, 128, 128], P('req', 'head'), may hold values from -6 to 6
- tok_latent: bfloat16 [6144, 576], P('req'), may hold values from -6 to 6
- w_uk: bfloat16 [128, 128, 512], P('head'), may hold values from -0.5 to 0.5
- w_uv: bfloat16 [128, 512, 128], P('head'), may hold values from -0.25 to 0.25
- pool: float32 [16, 64, 576], P('req', 'head'), may hold values from -6 to 6
- tenant_of_request: int32 [16], replicated, may hold values from 0 to 15
- slot_of_tenant: int32 [16], replicated, may hold values from 0 to 15, each once
Outputs:
- d_queries: bfloat16 [6144, 128, 192], P('req', 'head')
- d_tok_latent: bfloat16 [6144, 576], P(('req', 'head'))
- pool_grad: float32 [16, 64, 576], P('req', 'head')
The draws below stay inside these ranges and needn't reach their ends.
All inputs are finite; a program needn't handle non-finite values.
Results may differ from the reference program's by a relative error of at most 0.035.
Values may be sent and summed in bfloat16 or wider, within the bound.
No kernel may reach another device: no remote copies, remote signals or barrier semaphores. Data moves between devices by JAX's collectives and lax.ppermute only.
A program may use at most 64 MiB of HBM per device.

```python
import math
import jax
import jax.numpy as jnp
import numpy as np
from jax import lax

D_LAT = 512
D_ROPE = 64
D_NOPE = 128
D_V = 128
HEADS = 128
PREFIX = 64
SEQ = 384
REQUESTS = 16
TOKENS = 6144
SLOTS = 16
TENANTS = 16
LAT = 576


def draw_tok_latent(key, part):
    key = jax.random.fold_in(key, 3)
    shape = (TOKENS, D_LAT + D_ROPE)
    result = jnp.clip(jax.random.normal(key, shape, jnp.float32), -6.0, 6.0)
    return result.astype(jnp.bfloat16)


def draw_queries(key, part):
    key = jax.random.fold_in(key, 5)
    value_key = jax.random.fold_in(key, 0)
    shape = (TOKENS, HEADS, D_NOPE + D_ROPE)
    query_vals = jnp.clip(jax.random.normal(value_key, shape, jnp.float32), -6.0, 6.0)
    return query_vals.astype(jnp.bfloat16)


def set_ends(values, key, smallest, high):
    place = [jax.random.randint(jax.random.fold_in(key, axis), (), 0, length) for axis, length in enumerate(values.shape)]
    longest = values.shape.index(max(values.shape))
    next_to = place[:longest] + [(place[longest] + 1) % values.shape[longest]] + place[longest + 1:]
    return values.at[tuple(place)].set(smallest).at[tuple(next_to)].set(high)


def strengthened(entries, key, source, target, blocks, factor):
    def block_of(position):
        return (jnp.arange(entries.shape[position]) // (entries.shape[position] // blocks)).reshape((-1,) + (1,) * (entries.ndim - 1 - position))

    near = jax.random.permutation(key, blocks)[block_of(target)]
    second = (block_of(target) + blocks // 2) % blocks
    return jnp.where((block_of(source) == near) | (block_of(source) == second), factor * entries, entries)


def block_levels(own_key, shape, cuts, low, largest):
    def one(dim, blocks):
        draws = jax.random.uniform(jax.random.fold_in(jax.random.fold_in(own_key, 6), dim), (blocks,), jnp.float32, low / len(cuts), largest / len(cuts))
        return jnp.repeat(jnp.exp(draws), shape[dim] // blocks).reshape((-1,) + (1,) * (len(shape) - dim - 1))

    gain = one(*cuts[0])
    for cut in cuts[1:]:
        gain = gain * one(*cut)
    return gain


def cumulative_ranks(amount, lean):
    portions = [(1 << 20) // math.isqrt(rank ** lean) + 1 for rank in range(1, amount + 1)]
    deviation = 1 + sum(portions) // (1 << 30)
    return np.cumsum(np.array([max(1, weight // deviation) for weight in portions]))


def ranked_ids(rng, dims, amount, skew):
    grid = cumulative_ranks(amount, skew)
    ticket = jax.random.randint(jax.random.fold_in(rng, 1), dims, 0, int(grid[amount - 1]))
    rank = jnp.searchsorted(jnp.asarray(grid, jnp.int32), ticket, side="right")
    return jax.random.permutation(jax.random.fold_in(rng, 2), amount)[rank].astype(jnp.int32)


def centred(rng, dims, deviation, limit, cuts=(), held_as=jnp.bfloat16):
    drawn = jax.random.normal(rng, dims, jnp.float32) * deviation
    if len(cuts) > 0:
        drawn = block_levels(rng, dims, cuts, -0.22, 0.18) * drawn
    return jnp.clip(drawn, min=-limit, max=limit).astype(held_as)


def heavy_noise(key, shape, spread, bound, pieces, heavy, held_as=jnp.bfloat16):
    drawn = spread * jax.random.normal(key, shape, jnp.float32)
    if pieces:
        drawn = drawn * block_levels(key, shape, pieces, -0.22, 0.18)
    return jnp.clip(strengthened(drawn, jax.random.fold_in(key, 3), *heavy), -bound, bound).astype(held_as)


def setup_inputs(seed: int = 0) -> dict:
    arg_keys = jax.random.split(jax.random.key(seed), 9)
    queries = draw_queries(jax.random.fold_in(arg_keys[8], 71), 0)
    d_out = heavy_noise(arg_keys[1], (TOKENS, HEADS, D_V), 1.0, 6.0, ((0, 16), (1, 32)), (1, 0, 32, 2.75))
    tok_latent = draw_tok_latent(jax.random.fold_in(arg_keys[8], 71), 0)
    w_uk = centred(arg_keys[3], (HEADS, D_NOPE, D_LAT), D_NOPE ** -0.5, 0.5, ((0, 32),))
    w_uv = centred(arg_keys[4], (HEADS, D_LAT, D_V), D_LAT ** -0.5, 0.25, ((0, 32),))
    pool = centred(arg_keys[5], (SLOTS, PREFIX, LAT), 1.0, 6.0, ((0, 16), (1, 32)), jnp.float32)
    tenant_of_request = set_ends(ranked_ids(arg_keys[6], (REQUESTS,), TENANTS, 2), jax.random.fold_in(arg_keys[6], 3), 0, TENANTS - 1).astype(jnp.int32)
    slot_of_tenant = jax.random.permutation(arg_keys[7], SLOTS).astype(jnp.int32)
    return dict(queries=queries, d_out=d_out, tok_latent=tok_latent, w_uk=w_uk, w_uv=w_uv, pool=pool, tenant_of_request=tenant_of_request, slot_of_tenant=slot_of_tenant)


def head_backward(all_keys, query_head, dout_head, up_key, up_value, score_scale):
    query_lat = jnp.dot(query_head[:, :D_NOPE], up_key, preferred_element_type=jnp.float32).astype(jnp.bfloat16)
    query_full = jnp.concatenate([query_lat, query_head[:, D_NOPE:]], axis=1)
    scores = jnp.dot(query_full, all_keys.T, preferred_element_type=jnp.float32) * score_scale
    row_pos = jnp.arange(SEQ, dtype=jnp.int32)[:, None]
    col_pos = jnp.arange(PREFIX + SEQ, dtype=jnp.int32)[None, :]
    visible = (col_pos < PREFIX) | (col_pos - PREFIX <= row_pos)
    scores = jnp.where(visible, scores, -1e30)
    row_top = jnp.max(scores, axis=1, keepdims=True)
    exp_terms = jnp.where(visible, jnp.exp(scores - row_top), 0.0)
    attn_probs = exp_terms / jnp.sum(exp_terms, axis=1, keepdims=True)
    probs_half = attn_probs.astype(jnp.bfloat16)
    values = all_keys[:, :D_LAT]
    out_lat = jnp.dot(probs_half, values, preferred_element_type=jnp.float32)
    dout_lat = jnp.dot(dout_head, up_value.T, preferred_element_type=jnp.float32).astype(jnp.bfloat16)
    d_probs = jnp.dot(dout_lat, values.T, preferred_element_type=jnp.float32)
    delta_row = jnp.sum(dout_lat.astype(jnp.float32) * out_lat, axis=1, keepdims=True)
    d_scores = (attn_probs * (d_probs - delta_row) * score_scale).astype(jnp.bfloat16)
    key_grad = jnp.dot(d_scores.T, query_full, preferred_element_type=jnp.float32)
    value_grad = jnp.dot(probs_half.T, dout_lat, preferred_element_type=jnp.float32)
    key_grad = jnp.concatenate([key_grad[:, :D_LAT] + value_grad, key_grad[:, D_LAT:]], axis=1)
    d_query = jnp.dot(d_scores, all_keys, preferred_element_type=jnp.float32)
    d_nope = jnp.dot(d_query[:, :D_LAT].astype(jnp.bfloat16), up_key.T, preferred_element_type=jnp.float32)
    d_head = jnp.concatenate([d_nope, d_query[:, D_LAT:]], axis=1).astype(jnp.bfloat16)
    return key_grad, d_head


def reference(queries, d_out, tok_latent, w_uk, w_uv, pool, tenant_of_request, slot_of_tenant):
    score_scale = float(D_NOPE + D_ROPE) ** -0.5
    slot_ids = slot_of_tenant[tenant_of_request]

    def one_request(pool_sum, request):
        begin = (request * SEQ).astype(jnp.int32)
        query_req = lax.dynamic_slice_in_dim(queries, begin, SEQ, 0)
        dout_req = lax.dynamic_slice_in_dim(d_out, begin, SEQ, 0)
        latent_req = lax.dynamic_slice_in_dim(tok_latent, begin, SEQ, 0)
        my_slot = slot_ids[request]
        prefix = lax.dynamic_index_in_dim(pool, my_slot, 0, keepdims=False).astype(jnp.bfloat16)
        all_keys = jnp.concatenate([prefix, latent_req], axis=0)

        def per_head(key_total, head_number):
            key_grad, d_head = head_backward(all_keys, query_req[:, head_number], dout_req[:, head_number], w_uk[head_number], w_uv[head_number], score_scale)
            return key_total + key_grad, d_head

        start_total = jnp.zeros((PREFIX + SEQ, D_LAT + D_ROPE), jnp.float32)
        key_total, dquery_heads = lax.scan(per_head, start_total, jnp.arange(HEADS, dtype=jnp.int32))
        owned_slot = (jnp.arange(SLOTS, dtype=jnp.int32) == my_slot)[:, None, None]
        pool_sum = pool_sum + jnp.where(owned_slot, key_total[:PREFIX][None], 0.0)
        return pool_sum, (jnp.transpose(dquery_heads, (1, 0, 2)), key_total[PREFIX:].astype(jnp.bfloat16))

    start_pool = jnp.zeros((SLOTS, PREFIX, D_LAT + D_ROPE), jnp.float32)
    pool_grad, (dquery_all, dtoken_all) = lax.scan(one_request, start_pool, jnp.arange(REQUESTS, dtype=jnp.int32))
    d_queries = dquery_all.reshape(TOKENS, HEADS, D_NOPE + D_ROPE)
    d_tok_latent = dtoken_all.reshape(TOKENS, D_LAT + D_ROPE)
    return d_queries, d_tok_latent, pool_grad
```

```python
import jax
import jax.numpy as jnp
from jax import lax
from jax.sharding import PartitionSpec as P

D_LAT = 512
D_ROPE = 64
D_NOPE = 128
CHUNK = 16
bf16 = jnp.bfloat16
f32 = jnp.float32


def shards(queries, d_out, tok_latent, w_uk, w_uv, pool, tenant_of_request, slot_of_tenant):
    score_scale = float(D_NOPE + D_ROPE) ** (-0.5)
    heads = lax.axis_size("head")
    reqs = lax.axis_size("req")
    req_place = lax.axis_index("req")
    slot_ids = slot_of_tenant[tenant_of_request]
    my_slot = lax.dynamic_index_in_dim(slot_ids, req_place, 0, keepdims=False)
    lat = pool.shape[2]
    pre = pool.shape[1]
    seq = queries.shape[0]
    tok = seq // heads

    with jax.named_scope("fetch_slots"):
        mine = jnp.broadcast_to(pool.astype(bf16), (reqs, pre, lat))
        all_slots = lax.all_to_all(mine, "req", 0, 0)
    with jax.named_scope("spread_prefix"):
        rows = lax.dynamic_index_in_dim(all_slots, my_slot, 0, keepdims=True)
        prefix = lax.all_to_all(jnp.broadcast_to(rows, (heads, pre, lat)), "head", 0, 0)

    with jax.named_scope("keys"):
        tokens = tok_latent.reshape(heads, tok, lat)
        spare = jnp.zeros((heads, CHUNK - pre - tok, lat), bf16)
        keys = jnp.concatenate([prefix, tokens, spare], axis=1).reshape(heads * CHUNK, lat)
        latents = keys[:, :D_LAT]
    key_h = jnp.einsum("kl,hnl->hkn", latents, w_uk, preferred_element_type=f32).astype(bf16)
    val_h = jnp.einsum("kl,hlv->hkv", latents, w_uv, preferred_element_type=f32).astype(bf16)
    q = jnp.transpose(queries, (1, 0, 2))
    do = jnp.transpose(d_out, (1, 0, 2))
    n_h = q.shape[0]
    rope = jnp.broadcast_to(keys[None, :, D_LAT:], (n_h, heads * CHUNK, D_ROPE))
    key_full = jnp.concatenate([key_h, rope], axis=2)
    scores = jnp.einsum("hsn,hkn->hsk", q, key_full, preferred_element_type=f32) * score_scale
    place = jnp.arange(heads * CHUNK, dtype=jnp.int32)
    chunk, inner = place // CHUNK, place % CHUNK
    number = chunk * tok + inner - pre
    earliest = jnp.where(inner < pre, 0, jnp.where(inner < pre + tok, number, seq))
    visible = (earliest[None, :] <= jnp.arange(seq, dtype=jnp.int32)[:, None])[None]
    scores = jnp.where(visible, scores, -1e30)
    top = jnp.max(scores, axis=2, keepdims=True)
    terms = jnp.where(visible, jnp.exp(scores - top), 0.0)
    probs = terms / jnp.sum(terms, axis=2, keepdims=True)
    probs_half = probs.astype(bf16)
    d_probs = jnp.einsum("hsv,hkv->hsk", do, val_h, preferred_element_type=f32)
    delta = jnp.sum(probs * d_probs, axis=2, keepdims=True)
    d_scores = (probs * (d_probs - delta) * score_scale).astype(bf16)
    d_queries = jnp.einsum("hsk,hkn->shn", d_scores, key_full, preferred_element_type=f32).astype(bf16)
    ds_q = jnp.einsum("hsk,hsn->hkn", d_scores, q, preferred_element_type=f32)
    p_do = jnp.einsum("hsk,hsv->hkv", probs_half, do, preferred_element_type=f32).astype(bf16)
    lat_grad = jnp.einsum("hkn,hnl->kl", ds_q[:, :, :D_NOPE].astype(bf16), w_uk, preferred_element_type=f32)
    lat_grad += jnp.einsum("hkv,hlv->kl", p_do, w_uv, preferred_element_type=f32)
    rope_grad = jnp.sum(ds_q[:, :, D_NOPE:], axis=0)
    key_grad = jnp.concatenate([lat_grad, rope_grad], axis=1).astype(bf16)

    with jax.named_scope("sum_heads"):
        parts = lax.all_to_all(key_grad.reshape(heads, CHUNK, lat), "head", 0, 0)
        share = jnp.sum(parts.astype(f32), axis=0)
    token_grad = share[pre : pre + tok].astype(bf16)
    with jax.named_scope("sum_slots"):
        sent = jnp.broadcast_to(share[:pre].astype(bf16)[None], (reqs, pre, lat))
        given = lax.all_to_all(sent, "req", 0, 0)
        owned = (slot_ids == req_place)[:, None, None]
        pool_grad = jnp.sum(jnp.where(owned, given.astype(f32), 0.0), axis=0, keepdims=True)
    return d_queries, token_grad, pool_grad


def solution(mesh):
    return jax.shard_map(
        shards,
        mesh=mesh,
        in_specs=(
            P("req", "head", None),
            P("req", "head", None),
            P("req", None),
            P("head", None, None),
            P("head", None, None),
            P("req", "head", None),
            P(),
            P(),
        ),
        out_specs=(P("req", "head", None), P(("req", "head"), None), P("req", "head", None)),
        check_vma=False,
    )
```

```python
import jax
import jax.numpy as jnp
from jax import lax
from jax.experimental import pallas as pl
from jax.experimental.pallas import tpu as pltpu
from jax.sharding import PartitionSpec as P

D_LAT = 512
D_ROPE = 64
D_NOPE = 128
SCALE = float(D_NOPE + D_ROPE) ** (-0.5)
bf16 = jnp.bfloat16
f32 = jnp.float32
CHUNK = 16
IN_VMEM = pl.BlockSpec(memory_space=pltpu.VMEM)
PARAMS = pltpu.CompilerParams(vmem_limit_bytes=24 * 1024 * 1024)


def dot(a, b):
    return jnp.dot(a, b, preferred_element_type=f32)


def dot_nt(a, b):
    return lax.dot_general(a, b, (((1,), (1,)), ((), ())), preferred_element_type=f32)


def dot_tn(a, b):
    return lax.dot_general(a, b, (((0,), (0,)), ((), ())), preferred_element_type=f32)


def token_scores(qt_ref, do_ref, tok_ref, uk_ref, uv_ref, e_ref, dp_ref, key_ref, stat_ref, both_ref):
    both_ref[:D_NOPE] = uk_ref[...]
    both_ref[D_NOPE:] = uv_ref[...].T
    made = dot_nt(tok_ref[:, :D_LAT], both_ref[...]).astype(bf16)
    key = jnp.concatenate([made[:, :D_NOPE], tok_ref[:, D_LAT:]], axis=1)
    key_ref[...] = key
    scores = dot(key, qt_ref[...]) * SCALE
    row = lax.broadcasted_iota(jnp.int32, scores.shape, 0)
    col = lax.broadcasted_iota(jnp.int32, scores.shape, 1)
    scores = jnp.where(row <= col, scores, -1e30)
    top = jnp.max(scores, axis=0, keepdims=True)
    terms = jnp.where(row <= col, jnp.exp(scores - top), 0.0)
    d_probs = dot_nt(made[:, D_NOPE:], do_ref[...])
    e_ref[...] = terms
    dp_ref[...] = d_probs
    stat_ref[0:1] = top
    stat_ref[1:2] = jnp.sum(terms, axis=0, keepdims=True)
    stat_ref[2:3] = jnp.sum(terms * d_probs, axis=0, keepdims=True)


def key_grads(qt_ref, do_ref, pre_ref, both_ref, e_ref, dp_ref, stat_ref, grad_ref, ds_ref, key_ref, tok_acc, pre_acc):
    n_h = qt_ref.shape[0]
    n_pre = pre_ref.shape[0]
    width = both_ref.shape[1]
    both = both_ref[...].reshape(n_h * width, D_LAT)
    made = dot_nt(pre_ref[:, :D_LAT], both).astype(bf16)
    sides = []
    rope = None
    for h in range(n_h):
        key = jnp.concatenate([made[:, h * width : h * width + D_NOPE], pre_ref[:, D_LAT:]], axis=1)
        key_ref[h] = key
        val = made[:, h * width + D_NOPE : (h + 1) * width]
        qt = qt_ref[h]
        do = do_ref[h]
        scores = dot(key, qt) * SCALE
        d_probs = dot_nt(val, do)
        tok_top = stat_ref[h, 0:1]
        top = jnp.maximum(tok_top, jnp.max(scores, axis=0, keepdims=True))
        terms = jnp.exp(scores - top)
        shrink = jnp.exp(tok_top - top)
        inverse = 1.0 / (shrink * stat_ref[h, 1:2] + jnp.sum(terms, axis=0, keepdims=True))
        pre_probs = terms * inverse
        factor = shrink * inverse
        delta = factor * stat_ref[h, 2:3] + jnp.sum(pre_probs * d_probs, axis=0, keepdims=True)
        tok_probs = e_ref[h] * factor
        ds_ref[h, :n_pre] = (pre_probs * (d_probs - delta) * SCALE).astype(bf16)
        ds_ref[h, n_pre:] = (tok_probs * (dp_ref[h] - delta) * SCALE).astype(bf16)
        probs = jnp.concatenate([pre_probs.astype(bf16), tok_probs.astype(bf16)], axis=0)
        ds_q = dot_nt(ds_ref[h], qt)
        sides += [ds_q[:, :D_NOPE].astype(bf16), dot(probs, do).astype(bf16)]
        rope = ds_q[:, D_NOPE:] if rope is None else rope + ds_q[:, D_NOPE:]
    lat = dot(jnp.concatenate(sides, axis=1), both)
    pre_acc[:, :D_LAT] = lat[:n_pre]
    pre_acc[:, D_LAT:] = rope[:n_pre]
    tok_acc[:, :D_LAT] = lat[n_pre:]
    tok_acc[:, D_LAT:] = rope[n_pre:]
    heads, chunk, wide = grad_ref.shape
    pre = n_pre // heads
    tok = tok_acc.shape[0] // heads
    spare = jnp.zeros((chunk - pre - tok, wide), f32)
    for i in range(heads):
        piece = [pre_acc[i * pre : (i + 1) * pre], tok_acc[i * tok : (i + 1) * tok], spare]
        grad_ref[i] = jnp.concatenate(piece, axis=0).astype(bf16)


def query_grads(tok_key_ref, pre_key_ref, ds_ref, out_ref):
    key = jnp.concatenate([pre_key_ref[...], tok_key_ref[...]], axis=0)
    out_ref[...] = dot_tn(key, ds_ref[...]).astype(bf16)


def per_head(*shape):
    return pl.BlockSpec((None, *shape), lambda h: (h, 0, 0))


def shared(*shape):
    return pl.BlockSpec(shape, lambda h: (0, 0))


def struct(shape, dtype):
    return jax.ShapeDtypeStruct(shape, dtype)


def cost(flops, nbytes, exps=0):
    return pl.CostEstimate(flops=int(flops), bytes_accessed=int(nbytes), transcendentals=int(exps))


def shards(queries, d_out, tok_latent, w_uk, w_uv, pool, tenant_of_request, slot_of_tenant):
    heads = lax.axis_size("head")
    reqs = lax.axis_size("req")
    req_place = lax.axis_index("req")
    slot_ids = slot_of_tenant[tenant_of_request]
    my_slot = lax.dynamic_index_in_dim(slot_ids, req_place, 0, keepdims=False)
    lat = pool.shape[2]
    pre = pool.shape[1]
    seq, n_h, d_q = queries.shape
    d_v = d_out.shape[2]
    tok = seq // heads
    n_pre = pre * heads

    with jax.named_scope("fetch_slots"):
        all_slots = lax.all_to_all(jnp.broadcast_to(pool, (reqs, pre, lat)), "req", 0, 0)

    q_t = jnp.transpose(queries, (1, 2, 0))
    do = jnp.transpose(d_out, (1, 0, 2))
    wide = D_NOPE + d_v
    with jax.named_scope("token_scores"):
        terms, d_probs, tok_key, stats, both = pl.pallas_call(
            token_scores,
            grid=(n_h,),
            in_specs=[per_head(d_q, seq), per_head(seq, d_v), shared(seq, lat), per_head(D_NOPE, D_LAT), per_head(D_LAT, d_v)],
            out_specs=[per_head(seq, seq), per_head(seq, seq), per_head(seq, d_q), per_head(8, seq), per_head(wide, D_LAT)],
            out_shape=[
                struct((n_h, seq, seq), f32),
                struct((n_h, seq, seq), f32),
                struct((n_h, seq, d_q), bf16),
                struct((n_h, 8, seq), f32),
                struct((n_h, wide, D_LAT), bf16),
            ],
            compiler_params=PARAMS,
            cost_estimate=cost(n_h * 2.0e8, 8e6, n_h * seq * seq),
        )(q_t, do, tok_latent, w_uk, w_uv)

    with jax.named_scope("spread_prefix"):
        rows = lax.dynamic_index_in_dim(all_slots, my_slot, 0, keepdims=True).astype(bf16)
        prefix = lax.all_to_all(jnp.broadcast_to(rows, (heads, pre, lat)), "head", 0, 0)
        prefix = prefix.reshape(n_pre, lat)

    with jax.named_scope("key_grads"):
        grads, d_scores, pre_key = pl.pallas_call(
            key_grads,
            in_specs=[IN_VMEM] * 7,
            out_specs=[IN_VMEM] * 3,
            out_shape=[
                struct((heads, CHUNK, lat), bf16),
                struct((n_h, n_pre + seq, seq), bf16),
                struct((n_h, n_pre, d_q), bf16),
            ],
            scratch_shapes=[pltpu.VMEM((seq, lat), f32), pltpu.VMEM((n_pre, lat), f32)],
            compiler_params=PARAMS,
            cost_estimate=cost(n_h * 2.5e8, 8e6, n_h * seq * n_pre),
        )(q_t, do, prefix, both, terms, d_probs, stats)

    with jax.named_scope("sum_heads"):
        parts = lax.all_to_all(grads, "head", 0, 0)

    with jax.named_scope("query_grads"):
        d_q_t = pl.pallas_call(
            query_grads,
            grid=(n_h,),
            in_specs=[per_head(seq, d_q), per_head(n_pre, d_q), per_head(n_pre + seq, seq)],
            out_specs=per_head(d_q, seq),
            out_shape=struct((n_h, d_q, seq), bf16),
            compiler_params=PARAMS,
            cost_estimate=cost(n_h * 8e7, 3e6),
        )(tok_key, pre_key, d_scores)
        d_queries = jnp.transpose(d_q_t, (2, 0, 1))

    with jax.named_scope("sum_slots"):
        share = jnp.sum(parts.astype(f32), axis=0)
        token_grad = share[pre : pre + tok].astype(bf16)
        given = lax.all_to_all(jnp.broadcast_to(share[:pre].astype(bf16)[None], (reqs, pre, lat)), "req", 0, 0)
        owned = (slot_ids == req_place)[:, None, None]
        pool_grad = jnp.sum(jnp.where(owned, given.astype(f32), 0.0), axis=0, keepdims=True)
    return d_queries, token_grad, pool_grad


def solution(mesh):
    return jax.shard_map(
        shards,
        mesh=mesh,
        in_specs=(
            P("req", "head", None),
            P("req", "head", None),
            P("req", None),
            P("head", None, None),
            P("head", None, None),
            P("req", "head", None),
            P(),
            P(),
        ),
        out_specs=(P("req", "head", None), P(("req", "head"), None), P("req", "head", None)),
        check_vma=False,
    )
```

```python
import jax
import jax.numpy as jnp
from jax import lax
from jax.experimental import pallas as pl
from jax.experimental.pallas import tpu as pltpu
from jax.sharding import PartitionSpec as P

D_LAT = 512
D_ROPE = 64
D_NOPE = 128
SCALE = float(D_NOPE + D_ROPE) ** (-0.5)
bf16 = jnp.bfloat16
f32 = jnp.float32
CHUNK = 16
ANYWHERE = pl.BlockSpec(memory_space=pl.ANY)
IN_VMEM = pl.BlockSpec(memory_space=pltpu.VMEM)
PARAMS = pltpu.CompilerParams(vmem_limit_bytes=56 * 1024 * 1024)


def dot(a, b):
    return jnp.dot(a, b, preferred_element_type=f32)


def dot_nt(a, b):
    return lax.dot_general(a, b, (((1,), (1,)), ((), ())), preferred_element_type=f32)


def dot_tn(a, b):
    return lax.dot_general(a, b, (((0,), (0,)), ((), ())), preferred_element_type=f32)


def token_scores(qt_ref, do_ref, tokt_ref, uk_ref, uv_ref, e_ref, dp_ref, key_ref, stat_ref, both_ref, tok_ref):
    @pl.when(pl.program_id(0) == 0)
    def _():
        tok_ref[...] = tokt_ref[...].T

    both_ref[:D_NOPE] = uk_ref[...]
    both_ref[D_NOPE:] = uv_ref[...].T
    made = dot_nt(tok_ref[:, :D_LAT], both_ref[...]).astype(bf16)
    key = jnp.concatenate([made[:, :D_NOPE], tok_ref[:, D_LAT:]], axis=1)
    key_ref[...] = key
    scores = dot(key, qt_ref[...]) * SCALE
    row = lax.broadcasted_iota(jnp.int32, scores.shape, 0)
    col = lax.broadcasted_iota(jnp.int32, scores.shape, 1)
    scores = jnp.where(row <= col, scores, -1e30)
    top = jnp.max(scores, axis=0, keepdims=True)
    terms = jnp.where(row <= col, jnp.exp(scores - top), 0.0)
    d_probs = dot_nt(made[:, D_NOPE:], do_ref[...])
    e_ref[...] = terms
    dp_ref[...] = d_probs
    stat_ref[0:1] = top
    stat_ref[1:2] = jnp.sum(terms, axis=0, keepdims=True)
    stat_ref[2:3] = jnp.sum(terms * d_probs, axis=0, keepdims=True)


def key_grads(
    qt_hbm, do_hbm, pre_hbm, both_hbm, e_hbm, dp_hbm, stat_hbm,
    grad_ref, ds_hbm, key_ref,
    qt_ref, do_ref, parts_ref, both_ref, e_ref, dp_ref, stat_ref, ds_ref, pre_f32, tok_acc, pre_acc, sems,
):
    n_h = qt_ref.shape[0]
    n_pre = pre_f32.shape[0]
    width = both_ref.shape[1]
    parts_in = pltpu.make_async_copy(pre_hbm, parts_ref, sems.at[0, 0])
    both_in = pltpu.make_async_copy(both_hbm, both_ref, sems.at[0, 1])
    stat_in = pltpu.make_async_copy(stat_hbm, stat_ref, sems.at[0, 2])
    for copy in (parts_in, both_in, stat_in):
        copy.start()
    arrays = ((qt_hbm, qt_ref), (do_hbm, do_ref), (e_hbm, e_ref), (dp_hbm, dp_ref))
    head_in = [
        [pltpu.make_async_copy(src.at[h], dst.at[h], sems.at[1 + h, i]) for i, (src, dst) in enumerate(arrays)]
        for h in range(n_h)
    ]
    head_out = [pltpu.make_async_copy(ds_ref.at[h], ds_hbm.at[h], sems.at[1 + h, 4]) for h in range(n_h)]
    for copies in head_in:
        for copy in copies:
            copy.start()
    heads, pre, wide = parts_ref.shape
    parts_in.wait()
    for i in range(heads):
        pre_f32[i * pre : (i + 1) * pre] = parts_ref[i].astype(f32)
    prefix = pre_f32[...].astype(bf16)
    both_in.wait()
    both = both_ref[...].reshape(n_h * width, D_LAT)
    made = dot_nt(prefix[:, :D_LAT], both).astype(bf16)
    stat_in.wait()
    sides = []
    rope = None
    for h in range(n_h):
        for copy in head_in[h]:
            copy.wait()
        key = jnp.concatenate([made[:, h * width : h * width + D_NOPE], prefix[:, D_LAT:]], axis=1)
        key_ref[h] = key
        val = made[:, h * width + D_NOPE : (h + 1) * width]
        qt = qt_ref[h]
        do = do_ref[h]
        scores = dot(key, qt) * SCALE
        d_probs = dot_nt(val, do)
        tok_top = stat_ref[h, 0:1]
        top = jnp.maximum(tok_top, jnp.max(scores, axis=0, keepdims=True))
        terms = jnp.exp(scores - top)
        shrink = jnp.exp(tok_top - top)
        inverse = 1.0 / (shrink * stat_ref[h, 1:2] + jnp.sum(terms, axis=0, keepdims=True))
        pre_probs = terms * inverse
        factor = shrink * inverse
        delta = factor * stat_ref[h, 2:3] + jnp.sum(pre_probs * d_probs, axis=0, keepdims=True)
        tok_probs = e_ref[h] * factor
        ds_ref[h, :n_pre] = (pre_probs * (d_probs - delta) * SCALE).astype(bf16)
        ds_ref[h, n_pre:] = (tok_probs * (dp_ref[h] - delta) * SCALE).astype(bf16)
        head_out[h].start()
        probs = jnp.concatenate([pre_probs.astype(bf16), tok_probs.astype(bf16)], axis=0)
        ds_q = dot_nt(ds_ref[h], qt)
        sides += [ds_q[:, :D_NOPE].astype(bf16), dot(probs, do).astype(bf16)]
        rope = ds_q[:, D_NOPE:] if rope is None else rope + ds_q[:, D_NOPE:]
    lat = dot(jnp.concatenate(sides, axis=1), both)
    pre_acc[:, :D_LAT] = lat[:n_pre]
    pre_acc[:, D_LAT:] = rope[:n_pre]
    tok_acc[:, :D_LAT] = lat[n_pre:]
    tok_acc[:, D_LAT:] = rope[n_pre:]
    chunk = grad_ref.shape[1]
    tok = tok_acc.shape[0] // heads
    spare = jnp.zeros((chunk - pre - tok, wide), f32)
    for i in range(heads):
        piece = [pre_acc[i * pre : (i + 1) * pre], tok_acc[i * tok : (i + 1) * tok], spare]
        grad_ref[i] = jnp.concatenate(piece, axis=0).astype(bf16)
    for copy in head_out:
        copy.wait()


def query_grads(tok_key_ref, pre_key_ref, ds_ref, out_ref):
    key = jnp.concatenate([pre_key_ref[...], tok_key_ref[...]], axis=0)
    out_ref[...] = dot_tn(key, ds_ref[...]).astype(bf16)


def per_head(*shape):
    return pl.BlockSpec((None, *shape), lambda h: (h, 0, 0))


def shared(*shape):
    return pl.BlockSpec(shape, lambda h: (0, 0))


def struct(shape, dtype):
    return jax.ShapeDtypeStruct(shape, dtype)


def cost(flops, nbytes, exps=0):
    return pl.CostEstimate(flops=int(flops), bytes_accessed=int(nbytes), transcendentals=int(exps))


def shards(queries, d_out, tok_latent, w_uk, w_uv, pool, tenant_of_request, slot_of_tenant):
    heads = lax.axis_size("head")
    reqs = lax.axis_size("req")
    req_place = lax.axis_index("req")
    slot_ids = slot_of_tenant[tenant_of_request]
    my_slot = lax.dynamic_index_in_dim(slot_ids, req_place, 0, keepdims=False)
    lat = pool.shape[2]
    pre = pool.shape[1]
    seq, n_h, d_q = queries.shape
    d_v = d_out.shape[2]
    tok = seq // heads
    n_pre = pre * heads

    with jax.named_scope("fetch_slots"):
        all_slots = lax.all_to_all(jnp.broadcast_to(pool, (reqs, pre, lat)), "req", 0, 0)

    q_t = jnp.transpose(queries, (1, 2, 0))
    do = jnp.transpose(d_out, (1, 0, 2))
    wide = D_NOPE + d_v
    with jax.named_scope("token_scores"):
        terms, d_probs, tok_key, stats, both = pl.pallas_call(
            token_scores,
            grid=(n_h,),
            in_specs=[per_head(d_q, seq), per_head(seq, d_v), shared(lat, seq), per_head(D_NOPE, D_LAT), per_head(D_LAT, d_v)],
            out_specs=[per_head(seq, seq), per_head(seq, seq), per_head(seq, d_q), per_head(8, seq), per_head(wide, D_LAT)],
            out_shape=[
                struct((n_h, seq, seq), f32),
                struct((n_h, seq, seq), f32),
                struct((n_h, seq, d_q), bf16),
                struct((n_h, 8, seq), f32),
                struct((n_h, wide, D_LAT), bf16),
            ],
            scratch_shapes=[pltpu.VMEM((seq, lat), bf16)],
            compiler_params=PARAMS,
            cost_estimate=cost(n_h * 2.0e8, 8e6, n_h * seq * seq),
        )(q_t, do, tok_latent.T, w_uk, w_uv)

    with jax.named_scope("spread_prefix"):
        rows = lax.dynamic_index_in_dim(all_slots, my_slot, 0, keepdims=True).astype(bf16)
        rows, stats = lax.optimization_barrier((rows, stats))
        prefix = lax.all_to_all(jnp.broadcast_to(rows, (heads, pre, lat)), "head", 0, 0)

    with jax.named_scope("key_grads"):
        grads, d_scores, pre_key = pl.pallas_call(
            key_grads,
            in_specs=[ANYWHERE] * 7,
            out_specs=[IN_VMEM, ANYWHERE, IN_VMEM],
            out_shape=[
                struct((heads, CHUNK, lat), bf16),
                struct((n_h, n_pre + seq, seq), bf16),
                struct((n_h, n_pre, d_q), bf16),
            ],
            scratch_shapes=[
                pltpu.VMEM((n_h, d_q, seq), bf16),
                pltpu.VMEM((n_h, seq, d_v), bf16),
                pltpu.VMEM((heads, pre, lat), bf16),
                pltpu.VMEM((n_h, wide, D_LAT), bf16),
                pltpu.VMEM((n_h, seq, seq), f32),
                pltpu.VMEM((n_h, seq, seq), f32),
                pltpu.VMEM((n_h, 8, seq), f32),
                pltpu.VMEM((n_h, n_pre + seq, seq), bf16),
                pltpu.VMEM((n_pre, lat), f32),
                pltpu.VMEM((seq, lat), f32),
                pltpu.VMEM((n_pre, lat), f32),
                pltpu.SemaphoreType.DMA((1 + n_h, 5)),
            ],
            compiler_params=PARAMS,
            cost_estimate=cost(n_h * 2.5e8, 8e6, n_h * seq * n_pre),
        )(q_t, do, prefix, both, terms, d_probs, stats)

    with jax.named_scope("sum_heads"):
        parts = lax.all_to_all(grads, "head", 0, 0)

    with jax.named_scope("query_grads"):
        d_q_t = pl.pallas_call(
            query_grads,
            grid=(n_h,),
            in_specs=[per_head(seq, d_q), per_head(n_pre, d_q), per_head(n_pre + seq, seq)],
            out_specs=per_head(d_q, seq),
            out_shape=struct((n_h, d_q, seq), bf16),
            compiler_params=PARAMS,
            cost_estimate=cost(n_h * 8e7, 3e6),
        )(tok_key, pre_key, d_scores)
        d_queries = jnp.transpose(d_q_t, (2, 0, 1))

    with jax.named_scope("sum_slots"):
        share = jnp.sum(parts.astype(f32), axis=0)
        token_grad = share[pre : pre + tok].astype(bf16)
        given = lax.all_to_all(jnp.broadcast_to(share[:pre].astype(bf16)[None], (reqs, pre, lat)), "req", 0, 0)
        owned = (slot_ids == req_place)[:, None, None]
        pool_grad = jnp.sum(jnp.where(owned, given.astype(f32), 0.0), axis=0, keepdims=True)
    return d_queries, token_grad, pool_grad


def solution(mesh):
    return jax.shard_map(
        shards,
        mesh=mesh,
        in_specs=(
            P("req", "head", None),
            P("req", "head", None),
            P("req", None),
            P("head", None, None),
            P("head", None, None),
            P("req", "head", None),
            P(),
            P(),
        ),
        out_specs=(P("req", "head", None), P(("req", "head"), None), P("req", "head", None)),
        check_vma=False,
    )
```

```python
import jax
import jax.numpy as jnp
from jax import lax
from jax.experimental import pallas as pl
from jax.experimental.pallas import tpu as pltpu
from jax.sharding import PartitionSpec as P

D_LAT = 512
D_ROPE = 64
D_NOPE = 128
SCALE = float(D_NOPE + D_ROPE) ** (-0.5)
bf16 = jnp.bfloat16
f32 = jnp.float32
CHUNK = 16
BLOCK = 128
REQ_FIRST = 10
HEAD_FIRST = 20
ANYWHERE = pl.BlockSpec(memory_space=pl.ANY)
IN_VMEM = pl.BlockSpec(memory_space=pltpu.VMEM)
PARAMS = pltpu.CompilerParams(vmem_limit_bytes=24 * 1024 * 1024)


def dot(a, b):
    return jnp.dot(a, b, preferred_element_type=f32)


def dot_nt(a, b):
    return lax.dot_general(a, b, (((1,), (1,)), ((), ())), preferred_element_type=f32)


def dot_tn(a, b):
    return lax.dot_general(a, b, (((0,), (0,)), ((), ())), preferred_element_type=f32)


def project_tokens(qt_hbm, do_hbm, tokt_hbm, uk_hbm, uv_hbm, held_ref, tokt_ref, uv_ref, sems):
    n_h, _, d_v = uv_ref.shape
    seq = tokt_ref.shape[1]
    rows = rows_held(n_h, seq)
    copies = [
        pltpu.make_async_copy(tokt_hbm, tokt_ref, sems.at[0]),
        pltpu.make_async_copy(uk_hbm, held_ref.at[rows["uk"]], sems.at[1]),
        pltpu.make_async_copy(uv_hbm, uv_ref, sems.at[2]),
        pltpu.make_async_copy(do_hbm, held_ref.at[rows["do"]], sems.at[3]),
        pltpu.make_async_copy(qt_hbm, held_ref.at[rows["q"], :seq], sems.at[4]),
    ]
    for copy in copies:
        copy.start()
    copies[0].wait()
    tok = tokt_ref[...].T
    copies[1].wait()
    held_ref[rows["key"]] = dot_nt(tok[:, :D_LAT], held_ref[rows["uk"]]).astype(bf16)
    copies[2].wait()
    at = rows["uv"].start
    for h in range(n_h):
        mine = slice(h * d_v, (h + 1) * d_v)
        held_ref[at + h * d_v : at + (h + 1) * d_v] = uv_ref[h].T
        held_ref[rows["val"], mine] = dot(tok[:, :D_LAT], uv_ref[h]).astype(bf16)
    for copy in copies[3:]:
        copy.wait()
    at = rows["q"].start
    held_ref[at : at + seq, seq : seq + D_ROPE] = tok[:, D_LAT:]


def rows_held(n_h, seq):
    sizes = dict(uk=n_h * D_NOPE, uv=n_h * D_NOPE, do=seq, key=seq, val=seq, q=n_h * (D_NOPE + D_ROPE))
    places, at = {}, 0
    for name, size in sizes.items():
        places[name] = slice(at, at + size)
        at += size
    return places


def key_grads(
    parts_ref, held_ref,
    own_ref, other_ref, ds_hbm, key_hbm,
    ds_ref, key_ref, probs_ref, pre_f32, tok_acc, pre_acc, sems,
):
    n_h, n_keys, seq = ds_ref.shape
    heads, pre, wide = parts_ref.shape
    n_pre = n_keys - seq
    d_q = D_NOPE + D_ROPE
    rows = rows_held(n_h, seq)
    at_q = rows["q"].start
    row = lax.broadcasted_iota(jnp.int32, (BLOCK, BLOCK), 0)
    col = lax.broadcasted_iota(jnp.int32, (BLOCK, BLOCK), 1)
    for i in range(heads):
        pre_f32[i * pre : (i + 1) * pre] = parts_ref[i].astype(f32)
    prefix = pre_f32[...].astype(bf16)
    uk = held_ref[rows["uk"]]
    uv = held_ref[rows["uv"]]
    pre_keys = dot_nt(prefix[:, :D_LAT], uk).astype(bf16)
    pre_vals = dot_nt(prefix[:, :D_LAT], uv).astype(bf16)
    key_rope = jnp.concatenate([prefix[:, D_LAT:], held_ref[at_q : at_q + seq, seq : seq + D_ROPE]], axis=0)
    key_sides = []
    val_sides = []
    rope = None
    out = []
    for h in range(n_h):
        mine = slice(h * D_NOPE, (h + 1) * D_NOPE)
        q_rows = slice(at_q + h * d_q, at_q + (h + 1) * d_q)
        key_ref[h, :, :D_NOPE] = jnp.concatenate([pre_keys[:, mine], held_ref[rows["key"], mine]], axis=0)
        key_ref[h, :, D_NOPE:] = key_rope
        val = jnp.concatenate([pre_vals[:, mine], held_ref[rows["val"], mine]], axis=0)
        for at in range(0, seq, BLOCK):
            here = slice(at, at + BLOCK)
            seen = n_pre + at + BLOCK
            scores = dot(key_ref[h, :seen], held_ref[q_rows, here]) * SCALE
            edge = jnp.where(row <= col, scores[seen - BLOCK :], -1e30)
            scores = jnp.concatenate([scores[: seen - BLOCK], edge], axis=0)
            d_probs = dot_nt(val[:seen], held_ref[rows["do"], mine][here])
            terms = jnp.exp(scores - jnp.max(scores, axis=0, keepdims=True))
            probs = terms * (1.0 / jnp.sum(terms, axis=0, keepdims=True))
            delta = jnp.sum(probs * d_probs, axis=0, keepdims=True)
            probs_ref[h, :seen, here] = probs.astype(bf16)
            ds_ref[h, :seen, here] = (probs * (d_probs - delta) * SCALE).astype(bf16)
            if seen < n_keys:
                probs_ref[h, seen:, here] = jnp.zeros((n_keys - seen, BLOCK), bf16)
                ds_ref[h, seen:, here] = jnp.zeros((n_keys - seen, BLOCK), bf16)
        for i, (kept, target) in enumerate(((key_ref, key_hbm), (ds_ref, ds_hbm))):
            out.append(pltpu.make_async_copy(kept.at[h], target.at[h], sems.at[h, i]))
            out[-1].start()
        ds_q = dot_nt(ds_ref[h], held_ref[q_rows, :seq])
        key_sides.append(ds_q[:, :D_NOPE].astype(bf16))
        val_sides.append(dot(probs_ref[h], held_ref[rows["do"], mine]).astype(bf16))
        rope = ds_q[:, D_NOPE:] if rope is None else rope + ds_q[:, D_NOPE:]
    lat = dot(jnp.concatenate(key_sides, axis=1), uk) + dot(jnp.concatenate(val_sides, axis=1), uv)
    pre_acc[:, :D_LAT] = lat[:n_pre]
    pre_acc[:, D_LAT:] = rope[:n_pre]
    tok_acc[:, :D_LAT] = lat[n_pre:]
    tok_acc[:, D_LAT:] = rope[n_pre:]
    shares, chunk, _ = own_ref.shape
    tok = seq // heads
    spare = jnp.zeros((chunk - pre - tok, wide), f32)
    first_core = lax.rem(lax.axis_index("head"), 2) == 0
    for i in range(shares):
        pair = []
        for core in range(2):
            j = (HEAD_FIRST + 2 * i + core) % heads
            k = (2 * i + core) * pre
            piece = [pre_acc[k : k + pre], tok_acc[j * tok : (j + 1) * tok], spare]
            pair.append(jnp.concatenate(piece, axis=0))
        own_ref[i] = jnp.where(first_core, pair[0], pair[1]).astype(bf16)
        other_ref[i] = jnp.where(first_core, pair[1], pair[0]).astype(bf16)
    for copy in out:
        copy.wait()


def query_grads(key_ref, ds_ref, out_ref):
    out_ref[...] = dot_tn(key_ref[...], ds_ref[...]).astype(bf16)


def per_head(*shape):
    return pl.BlockSpec((None, *shape), lambda h: (h, 0, 0))


def keep(space, *arrays):
    return [pltpu.with_memory_space_constraint(x, space) for x in arrays]


def struct(shape, dtype):
    return jax.ShapeDtypeStruct(shape, dtype)


def cost(flops, nbytes, exps=0):
    return pl.CostEstimate(flops=int(flops), bytes_accessed=int(nbytes), transcendentals=int(exps))


def from_first(first, size):
    return [[(first + i) % size for i in range(size)]]


def shards(queries, d_out, tok_latent, w_uk, w_uv, pool, tenant_of_request, slot_of_tenant):
    heads = lax.axis_size("head")
    reqs = lax.axis_size("req")
    req_first = REQ_FIRST % reqs
    req_group = from_first(req_first, reqs)
    head_group = from_first(HEAD_FIRST % heads, heads)
    req_place = lax.axis_index("req")
    slot_ids = slot_of_tenant.at[tenant_of_request].get(mode="promise_in_bounds")
    my_slot = lax.dynamic_slice(slot_ids, (req_place,), (1,), allow_negative_indices=False)[0]
    lat = pool.shape[2]
    pre = pool.shape[1]
    seq, n_h, d_q = queries.shape
    d_v = d_out.shape[2]
    tok = seq // heads
    n_pre = pre * heads

    with jax.named_scope("fetch_slots"):
        mine = jnp.broadcast_to(pool, (reqs, pre, lat))
        all_slots = lax.all_to_all(mine, "req", 0, 0, axis_index_groups=req_group)

    q_t = jnp.transpose(queries, (1, 2, 0))
    with jax.named_scope("spread_prefix"):
        place = lax.rem(my_slot + (reqs - req_first), reqs)
        rows = lax.dynamic_slice(all_slots, (place, 0, 0), (1, pre, lat), allow_negative_indices=False).astype(bf16)
        rows, d_out = lax.optimization_barrier((rows, d_out))
        prefix = lax.all_to_all(jnp.broadcast_to(rows, (heads, pre, lat)), "head", 0, 0, axis_index_groups=head_group)

    with jax.named_scope("project_tokens"):
        n_rows = max(x.stop for x in rows_held(n_h, seq).values())
        inputs = q_t.reshape(n_h * d_q, seq), d_out.reshape(seq, n_h * d_v), tok_latent.T, w_uk.reshape(n_h * D_NOPE, D_LAT), w_uv
        held = pl.pallas_call(
            project_tokens,
            in_specs=[ANYWHERE] * 5,
            out_specs=IN_VMEM,
            out_shape=pltpu.VMEM((n_rows, D_LAT), bf16),
            scratch_shapes=[
                pltpu.VMEM((lat, seq), bf16),
                pltpu.VMEM((n_h, D_LAT, d_v), bf16),
                pltpu.SemaphoreType.DMA((5,)),
            ],
            compiler_params=PARAMS,
            cost_estimate=cost(n_h * 1.0e8, 5e6),
        )(*keep(pltpu.HBM, *inputs))

    with jax.named_scope("key_grads"):
        own, other, d_scores, keys = pl.pallas_call(
            key_grads,
            in_specs=[IN_VMEM] * 2,
            out_specs=[IN_VMEM, IN_VMEM, ANYWHERE, ANYWHERE],
            out_shape=[
                pltpu.HBM((heads // 2, CHUNK, lat), bf16),
                pltpu.HBM((heads // 2, CHUNK, lat), bf16),
                pltpu.HBM((n_h, n_pre + seq, seq), bf16),
                pltpu.HBM((n_h, n_pre + seq, d_q), bf16),
            ],
            scratch_shapes=[
                pltpu.VMEM((n_h, n_pre + seq, seq), bf16),
                pltpu.VMEM((n_h, n_pre + seq, d_q), bf16),
                pltpu.VMEM((n_h, n_pre + seq, seq), bf16),
                pltpu.VMEM((n_pre, lat), f32),
                pltpu.VMEM((seq, lat), f32),
                pltpu.VMEM((n_pre, lat), f32),
                pltpu.SemaphoreType.DMA((n_h, 2)),
            ],
            compiler_params=PARAMS,
            cost_estimate=cost(n_h * 2.5e8, 5e6, n_h * seq * seq),
        )(prefix, *keep(pltpu.VMEM, held))

    with jax.named_scope("sum_heads"):
        given = lax.ppermute(other, "head", [(i, i ^ 1) for i in range(heads)])
        summed = (own.astype(f32) + given.astype(f32)).astype(bf16)
        core_groups = [[i + core for i in head_group[0][::2]] for core in range(2)]
        parts = lax.all_to_all(summed, "head", 0, 0, axis_index_groups=core_groups)

    with jax.named_scope("query_grads"):
        d_q_t = pl.pallas_call(
            query_grads,
            grid=(n_h,),
            in_specs=[per_head(n_pre + seq, d_q), per_head(n_pre + seq, seq)],
            out_specs=per_head(d_q, seq),
            out_shape=struct((n_h, d_q, seq), bf16),
            compiler_params=PARAMS,
            cost_estimate=cost(n_h * 8e7, 3e6),
        )(*keep(pltpu.HBM, keys, d_scores))

    with jax.named_scope("sum_slots"):
        share = jnp.sum(parts.astype(f32), axis=0)
        token_grad = share[pre : pre + tok].astype(bf16)
        owned = jnp.roll(slot_ids, -req_first) == req_place
        sent, d_q_t, owned = lax.optimization_barrier((share[:pre].astype(bf16), d_q_t, owned))
        sent = jnp.broadcast_to(sent[None], (reqs, pre, lat))
        given = lax.all_to_all(sent, "req", 0, 0, axis_index_groups=req_group)
        pool_grad = jnp.sum(jnp.where(owned[:, None, None], given.astype(f32), 0.0), axis=0, keepdims=True)
    d_queries = jnp.transpose(d_q_t, (2, 0, 1))
    return d_queries, token_grad, pool_grad


def solution(mesh):
    return jax.shard_map(
        shards,
        mesh=mesh,
        in_specs=(
            P("req", "head", None),
            P("req", "head", None),
            P("req", None),
            P("head", None, None),
            P("head", None, None),
            P("req", "head", None),
            P(),
            P(),
        ),
        out_specs=(P("req", "head", None), P(("req", "head"), None), P("req", "head", None)),
        check_vma=False,
    )
```

```python
import jax
import jax.numpy as jnp
from jax import lax
from jax.experimental import pallas as pl
from jax.experimental.pallas import tpu as pltpu
from jax.sharding import PartitionSpec as P

D_LAT = 512
D_ROPE = 64
D_NOPE = 128
SCALE = float(D_NOPE + D_ROPE) ** (-0.5)
bf16 = jnp.bfloat16
f32 = jnp.float32
CHUNK = 16
BLOCK = 128
REQ_FIRST = 10
HEAD_FIRST = 20
SPREAD_FIRST = 20
ANYWHERE = pl.BlockSpec(memory_space=pl.ANY)
IN_VMEM = pl.BlockSpec(memory_space=pltpu.VMEM)
PARAMS = pltpu.CompilerParams(vmem_limit_bytes=24 * 1024 * 1024)


def dot(a, b):
    return jnp.dot(a, b, preferred_element_type=f32)


def dot_nt(a, b):
    return lax.dot_general(a, b, (((1,), (1,)), ((), ())), preferred_element_type=f32)


def dot_tn(a, b):
    return lax.dot_general(a, b, (((0,), (0,)), ((), ())), preferred_element_type=f32)


def project_tokens(qt_hbm, do_hbm, tokt_hbm, uk_hbm, uv_hbm, held_ref, tokt_ref, uv_ref, sems):
    n_h, _, d_v = uv_ref.shape
    seq = tokt_ref.shape[1]
    rows = rows_held(n_h, seq)
    copies = [
        pltpu.make_async_copy(tokt_hbm, tokt_ref, sems.at[0]),
        pltpu.make_async_copy(uk_hbm, held_ref.at[rows["uk"]], sems.at[1]),
        pltpu.make_async_copy(uv_hbm, uv_ref, sems.at[2]),
        pltpu.make_async_copy(do_hbm, held_ref.at[rows["do"]], sems.at[3]),
        pltpu.make_async_copy(qt_hbm, held_ref.at[rows["q"], :seq], sems.at[4]),
    ]
    for copy in copies:
        copy.start()
    copies[0].wait()
    tok = tokt_ref[...].T
    copies[1].wait()
    held_ref[rows["key"]] = dot_nt(tok[:, :D_LAT], held_ref[rows["uk"]]).astype(bf16)
    copies[2].wait()
    at = rows["uv"].start
    for h in range(n_h):
        mine = slice(h * d_v, (h + 1) * d_v)
        held_ref[at + h * d_v : at + (h + 1) * d_v] = uv_ref[h].T
        held_ref[rows["val"], mine] = dot(tok[:, :D_LAT], uv_ref[h]).astype(bf16)
    for copy in copies[3:]:
        copy.wait()
    at = rows["q"].start
    held_ref[at : at + seq, seq : seq + D_ROPE] = tok[:, D_LAT:]


def rows_held(n_h, seq):
    sizes = dict(uk=n_h * D_NOPE, uv=n_h * D_NOPE, do=seq, key=seq, val=seq, q=n_h * (D_NOPE + D_ROPE))
    places, at = {}, 0
    for name, size in sizes.items():
        places[name] = slice(at, at + size)
        at += size
    return places


def key_grads(
    parts_ref, held_ref,
    own_ref, other_ref, ds_hbm, key_hbm,
    ds_ref, key_ref, probs_ref, pre_f32, tok_acc, pre_acc, sems,
):
    n_h, n_keys, seq = ds_ref.shape
    heads, pre, wide = parts_ref.shape
    n_pre = n_keys - seq
    d_q = D_NOPE + D_ROPE
    rows = rows_held(n_h, seq)
    at_q = rows["q"].start
    row = lax.broadcasted_iota(jnp.int32, (BLOCK, BLOCK), 0)
    col = lax.broadcasted_iota(jnp.int32, (BLOCK, BLOCK), 1)
    for i in range(heads):
        pre_f32[i * pre : (i + 1) * pre] = parts_ref[i].astype(f32)
    prefix = pre_f32[...].astype(bf16)
    uk = held_ref[rows["uk"]]
    uv = held_ref[rows["uv"]]
    pre_keys = dot_nt(prefix[:, :D_LAT], uk).astype(bf16)
    pre_vals = dot_nt(prefix[:, :D_LAT], uv).astype(bf16)
    key_rope = jnp.concatenate([prefix[:, D_LAT:], held_ref[at_q : at_q + seq, seq : seq + D_ROPE]], axis=0)
    key_sides = []
    val_sides = []
    rope = None
    out = []
    for h in range(n_h):
        mine = slice(h * D_NOPE, (h + 1) * D_NOPE)
        q_rows = slice(at_q + h * d_q, at_q + (h + 1) * d_q)
        key_ref[h, :, :D_NOPE] = jnp.concatenate([pre_keys[:, mine], held_ref[rows["key"], mine]], axis=0)
        key_ref[h, :, D_NOPE:] = key_rope
        val = jnp.concatenate([pre_vals[:, mine], held_ref[rows["val"], mine]], axis=0)
        for at in range(0, seq, BLOCK):
            here = slice(at, at + BLOCK)
            seen = n_pre + at + BLOCK
            scores = dot(key_ref[h, :seen], held_ref[q_rows, here]) * SCALE
            edge = jnp.where(row <= col, scores[seen - BLOCK :], -1e30)
            scores = jnp.concatenate([scores[: seen - BLOCK], edge], axis=0)
            d_probs = dot_nt(val[:seen], held_ref[rows["do"], mine][here])
            terms = jnp.exp(scores - jnp.max(scores, axis=0, keepdims=True))
            probs = terms * (1.0 / jnp.sum(terms, axis=0, keepdims=True))
            delta = jnp.sum(probs * d_probs, axis=0, keepdims=True)
            probs_ref[h, :seen, here] = probs.astype(bf16)
            ds_ref[h, :seen, here] = (probs * (d_probs - delta) * SCALE).astype(bf16)
            if seen < n_keys:
                probs_ref[h, seen:, here] = jnp.zeros((n_keys - seen, BLOCK), bf16)
                ds_ref[h, seen:, here] = jnp.zeros((n_keys - seen, BLOCK), bf16)
        for i, (kept, target) in enumerate(((key_ref, key_hbm), (ds_ref, ds_hbm))):
            out.append(pltpu.make_async_copy(kept.at[h], target.at[h], sems.at[h, i]))
            out[-1].start()
        ds_q = dot_nt(ds_ref[h], held_ref[q_rows, :seq])
        key_sides.append(ds_q[:, :D_NOPE].astype(bf16))
        val_sides.append(dot(probs_ref[h], held_ref[rows["do"], mine]).astype(bf16))
        rope = ds_q[:, D_NOPE:] if rope is None else rope + ds_q[:, D_NOPE:]
    lat = dot(jnp.concatenate(key_sides, axis=1), uk) + dot(jnp.concatenate(val_sides, axis=1), uv)
    pre_acc[:, :D_LAT] = lat[:n_pre]
    pre_acc[:, D_LAT:] = rope[:n_pre]
    tok_acc[:, :D_LAT] = lat[n_pre:]
    tok_acc[:, D_LAT:] = rope[n_pre:]
    shares, chunk, _ = own_ref.shape
    tok = seq // heads
    spare = jnp.zeros((chunk - pre - tok, wide), f32)
    first_core = lax.rem(lax.axis_index("head"), 2) == 0
    for i in range(shares):
        pair = []
        for core in range(2):
            j = (HEAD_FIRST + 2 * i + core) % heads
            k = (2 * i + core) * pre
            piece = [pre_acc[k : k + pre], tok_acc[j * tok : (j + 1) * tok], spare]
            pair.append(jnp.concatenate(piece, axis=0))
        own_ref[i] = jnp.where(first_core, pair[0], pair[1]).astype(bf16)
        other_ref[i] = jnp.where(first_core, pair[1], pair[0]).astype(bf16)
    for copy in out:
        copy.wait()


def add_shares(own_ref, given_ref, out_ref):
    out_ref[...] = (own_ref[...].astype(f32) + given_ref[...].astype(f32)).astype(bf16)


def query_grads(key_ref, ds_ref, out_ref):
    out_ref[...] = dot_tn(key_ref[...], ds_ref[...]).astype(bf16)


def per_head(*shape):
    return pl.BlockSpec((None, *shape), lambda h: (h, 0, 0))


def keep(space, *arrays):
    return [pltpu.with_memory_space_constraint(x, space) for x in arrays]


def struct(shape, dtype):
    return jax.ShapeDtypeStruct(shape, dtype)


def cost(flops, nbytes, exps=0):
    return pl.CostEstimate(flops=int(flops), bytes_accessed=int(nbytes), transcendentals=int(exps))


def from_first(first, size):
    return [[(first + i) % size for i in range(size)]]


def shards(queries, d_out, tok_latent, w_uk, w_uv, pool, tenant_of_request, slot_of_tenant):
    heads = lax.axis_size("head")
    reqs = lax.axis_size("req")
    req_first = REQ_FIRST % reqs
    req_group = from_first(req_first, reqs)
    head_group = from_first(HEAD_FIRST % heads, heads)
    spread_group = from_first(SPREAD_FIRST % heads, heads)
    req_place = lax.axis_index("req")
    slot_ids = slot_of_tenant.at[tenant_of_request].get(mode="promise_in_bounds")
    my_slot = lax.dynamic_slice(slot_ids, (req_place,), (1,), allow_negative_indices=False)[0]
    lat = pool.shape[2]
    pre = pool.shape[1]
    seq, n_h, d_q = queries.shape
    d_v = d_out.shape[2]
    tok = seq // heads
    n_pre = pre * heads

    with jax.named_scope("fetch_slots"):
        mine = jnp.broadcast_to(pool, (reqs, pre, lat))
        all_slots = lax.all_to_all(mine, "req", 0, 0, axis_index_groups=req_group)

    q_t = jnp.transpose(queries, (1, 2, 0))
    with jax.named_scope("spread_prefix"):
        place = lax.rem(my_slot + (reqs - req_first), reqs)
        rows = lax.dynamic_slice(all_slots, (place, 0, 0), (1, pre, lat), allow_negative_indices=False).astype(bf16)
        rows, d_out = lax.optimization_barrier((rows, d_out))
        prefix = lax.all_to_all(jnp.broadcast_to(rows, (heads, pre, lat)), "head", 0, 0, axis_index_groups=spread_group)

    with jax.named_scope("project_tokens"):
        n_rows = max(x.stop for x in rows_held(n_h, seq).values())
        inputs = q_t.reshape(n_h * d_q, seq), d_out.reshape(seq, n_h * d_v), tok_latent.T, w_uk.reshape(n_h * D_NOPE, D_LAT), w_uv
        held = pl.pallas_call(
            project_tokens,
            in_specs=[ANYWHERE] * 5,
            out_specs=IN_VMEM,
            out_shape=pltpu.VMEM((n_rows, D_LAT), bf16),
            scratch_shapes=[
                pltpu.VMEM((lat, seq), bf16),
                pltpu.VMEM((n_h, D_LAT, d_v), bf16),
                pltpu.SemaphoreType.DMA((5,)),
            ],
            compiler_params=PARAMS,
            cost_estimate=cost(n_h * 1.0e8, 5e6),
        )(*keep(pltpu.HBM, *inputs))

    with jax.named_scope("key_grads"):
        own, other, d_scores, keys = pl.pallas_call(
            key_grads,
            in_specs=[IN_VMEM] * 2,
            out_specs=[IN_VMEM, IN_VMEM, ANYWHERE, ANYWHERE],
            out_shape=[
                pltpu.VMEM((heads // 2, CHUNK, lat), bf16),
                pltpu.HBM((heads // 2, CHUNK, lat), bf16),
                pltpu.HBM((n_h, n_pre + seq, seq), bf16),
                pltpu.HBM((n_h, n_pre + seq, d_q), bf16),
            ],
            scratch_shapes=[
                pltpu.VMEM((n_h, n_pre + seq, seq), bf16),
                pltpu.VMEM((n_h, n_pre + seq, d_q), bf16),
                pltpu.VMEM((n_h, n_pre + seq, seq), bf16),
                pltpu.VMEM((n_pre, lat), f32),
                pltpu.VMEM((seq, lat), f32),
                pltpu.VMEM((n_pre, lat), f32),
                pltpu.SemaphoreType.DMA((n_h, 2)),
            ],
            compiler_params=PARAMS,
            cost_estimate=cost(n_h * 2.5e8, 5e6, n_h * seq * seq),
        )(prefix, *keep(pltpu.VMEM, held))

    with jax.named_scope("sum_heads"):
        given = lax.ppermute(other, "head", [(i, i ^ 1) for i in range(heads)])
        summed = pl.pallas_call(
            add_shares,
            in_specs=[IN_VMEM] * 2,
            out_specs=IN_VMEM,
            out_shape=pltpu.HBM(own.shape, bf16),
            compiler_params=PARAMS,
            cost_estimate=cost(2e5, 1e6),
        )(*keep(pltpu.VMEM, own), given)
        core_groups = [[i + core for i in head_group[0][::2]] for core in range(2)]
        parts = lax.all_to_all(summed, "head", 0, 0, axis_index_groups=core_groups)

    with jax.named_scope("query_grads"):
        d_q_t = pl.pallas_call(
            query_grads,
            grid=(n_h,),
            in_specs=[per_head(n_pre + seq, d_q), per_head(n_pre + seq, seq)],
            out_specs=per_head(d_q, seq),
            out_shape=struct((n_h, d_q, seq), bf16),
            compiler_params=PARAMS,
            cost_estimate=cost(n_h * 8e7, 3e6),
        )(*keep(pltpu.HBM, keys, d_scores))

    with jax.named_scope("sum_slots"):
        share = jnp.sum(parts.astype(f32), axis=0)
        token_grad = share[pre : pre + tok].astype(bf16)
        owned = jnp.roll(slot_ids, -req_first) == req_place
        sent, d_q_t, owned = lax.optimization_barrier((share[:pre].astype(bf16), d_q_t, owned))
        sent = jnp.broadcast_to(sent[None], (reqs, pre, lat))
        given = lax.all_to_all(sent, "req", 0, 0, axis_index_groups=req_group)
        pool_grad = jnp.sum(jnp.where(owned[:, None, None], given.astype(f32), 0.0), axis=0, keepdims=True)
    d_queries = jnp.transpose(d_q_t, (2, 0, 1))
    return d_queries, token_grad, pool_grad


def solution(mesh):
    return jax.shard_map(
        shards,
        mesh=mesh,
        in_specs=(
            P("req", "head", None),
            P("req", "head", None),
            P("req", None),
            P("head", None, None),
            P("head", None, None),
            P("req", "head", None),
            P(),
            P(),
        ),
        out_specs=(P("req", "head", None), P(("req", "head"), None), P("req", "head", None)),
        check_vma=False,
    )
```

```python
import jax
import jax.numpy as jnp
from jax import lax
from jax.experimental import pallas as pl
from jax.experimental.pallas import tpu as pltpu
from jax.sharding import PartitionSpec as P

D_LAT = 512
D_ROPE = 64
D_NOPE = 128
SCALE = float(D_NOPE + D_ROPE) ** (-0.5)
bf16 = jnp.bfloat16
f32 = jnp.float32
CHUNK = 16
BLOCK = 128
REQ_FIRST = 10
HEAD_FIRST = 20
SPREAD_FIRST = 20
ANYWHERE = pl.BlockSpec(memory_space=pl.ANY)
IN_VMEM = pl.BlockSpec(memory_space=pltpu.VMEM)
PARAMS = pltpu.CompilerParams(vmem_limit_bytes=24 * 1024 * 1024)


def dot(a, b):
    return jnp.dot(a, b, preferred_element_type=f32)


def dot_nt(a, b):
    return lax.dot_general(a, b, (((1,), (1,)), ((), ())), preferred_element_type=f32)


def dot_tn(a, b):
    return lax.dot_general(a, b, (((0,), (0,)), ((), ())), preferred_element_type=f32)


def project_tokens(qt_hbm, do_hbm, tokt_hbm, uk_hbm, uv_hbm, held_ref, tokt_ref, uv_ref, sems):
    n_h, _, d_v = uv_ref.shape
    seq = tokt_ref.shape[1]
    rows = rows_held(n_h, seq)
    copies = [
        pltpu.make_async_copy(tokt_hbm, tokt_ref, sems.at[0]),
        pltpu.make_async_copy(uk_hbm, held_ref.at[rows["uk"]], sems.at[1]),
        pltpu.make_async_copy(uv_hbm, uv_ref, sems.at[2]),
        pltpu.make_async_copy(do_hbm, held_ref.at[rows["do"]], sems.at[3]),
        pltpu.make_async_copy(qt_hbm, held_ref.at[rows["q"], :seq], sems.at[4]),
    ]
    for copy in copies:
        copy.start()
    copies[0].wait()
    tok = tokt_ref[...].T
    copies[1].wait()
    held_ref[rows["key"]] = dot_nt(tok[:, :D_LAT], held_ref[rows["uk"]]).astype(bf16)
    copies[2].wait()
    at = rows["uv"].start
    for h in range(n_h):
        mine = slice(h * d_v, (h + 1) * d_v)
        held_ref[at + h * d_v : at + (h + 1) * d_v] = uv_ref[h].T
        held_ref[rows["val"], mine] = dot(tok[:, :D_LAT], uv_ref[h]).astype(bf16)
    for copy in copies[3:]:
        copy.wait()
    at = rows["q"].start
    held_ref[at : at + seq, seq : seq + D_ROPE] = tok[:, D_LAT:]


def rows_held(n_h, seq):
    sizes = dict(uk=n_h * D_NOPE, uv=n_h * D_NOPE, do=seq, key=seq, val=seq, q=n_h * (D_NOPE + D_ROPE))
    places, at = {}, 0
    for name, size in sizes.items():
        places[name] = slice(at, at + size)
        at += size
    return places


def key_grads(
    parts_ref, held_ref,
    own_ref, other_ref, ds_hbm, key_hbm,
    ds_ref, key_ref, probs_ref, pre_f32, tok_acc, pre_acc, sems,
):
    n_h, n_keys, seq = ds_ref.shape
    heads, pre, wide = parts_ref.shape
    n_pre = n_keys - seq
    d_q = D_NOPE + D_ROPE
    rows = rows_held(n_h, seq)
    at_q = rows["q"].start
    row = lax.broadcasted_iota(jnp.int32, (BLOCK, BLOCK), 0)
    col = lax.broadcasted_iota(jnp.int32, (BLOCK, BLOCK), 1)
    for i in range(heads):
        pre_f32[i * pre : (i + 1) * pre] = parts_ref[i].astype(f32)
    prefix = pre_f32[...].astype(bf16)
    uk = held_ref[rows["uk"]]
    uv = held_ref[rows["uv"]]
    pre_keys = dot_nt(prefix[:, :D_LAT], uk).astype(bf16)
    pre_vals = dot_nt(prefix[:, :D_LAT], uv).astype(bf16)
    key_rope = jnp.concatenate([prefix[:, D_LAT:], held_ref[at_q : at_q + seq, seq : seq + D_ROPE]], axis=0)
    key_sides = []
    val_sides = []
    rope = None
    out = []
    for h in range(n_h):
        mine = slice(h * D_NOPE, (h + 1) * D_NOPE)
        q_rows = slice(at_q + h * d_q, at_q + (h + 1) * d_q)
        key_ref[h, :, :D_NOPE] = jnp.concatenate([pre_keys[:, mine], held_ref[rows["key"], mine]], axis=0)
        key_ref[h, :, D_NOPE:] = key_rope
        val = jnp.concatenate([pre_vals[:, mine], held_ref[rows["val"], mine]], axis=0)
        for at in range(0, seq, BLOCK):
            here = slice(at, at + BLOCK)
            seen = n_pre + at + BLOCK
            scores = dot(key_ref[h, :seen], held_ref[q_rows, here]) * SCALE
            edge = jnp.where(row <= col, scores[seen - BLOCK :], -1e30)
            scores = jnp.concatenate([scores[: seen - BLOCK], edge], axis=0)
            d_probs = dot_nt(val[:seen], held_ref[rows["do"], mine][here])
            terms = jnp.exp(scores - jnp.max(scores, axis=0, keepdims=True))
            probs = terms * (1.0 / jnp.sum(terms, axis=0, keepdims=True))
            delta = jnp.sum(probs * d_probs, axis=0, keepdims=True)
            probs_ref[h, :seen, here] = probs.astype(bf16)
            ds_ref[h, :seen, here] = (probs * (d_probs - delta) * SCALE).astype(bf16)
            if seen < n_keys:
                probs_ref[h, seen:, here] = jnp.zeros((n_keys - seen, BLOCK), bf16)
                ds_ref[h, seen:, here] = jnp.zeros((n_keys - seen, BLOCK), bf16)
        for i, (kept, target) in enumerate(((key_ref, key_hbm), (ds_ref, ds_hbm))):
            out.append(pltpu.make_async_copy(kept.at[h], target.at[h], sems.at[h, i]))
            out[-1].start()
        ds_q = dot_nt(ds_ref[h], held_ref[q_rows, :seq])
        key_sides.append(ds_q[:, :D_NOPE].astype(bf16))
        val_sides.append(dot(probs_ref[h], held_ref[rows["do"], mine]).astype(bf16))
        rope = ds_q[:, D_NOPE:] if rope is None else rope + ds_q[:, D_NOPE:]
    lat = dot(jnp.concatenate(key_sides, axis=1), uk) + dot(jnp.concatenate(val_sides, axis=1), uv)
    pre_acc[:, :D_LAT] = lat[:n_pre]
    pre_acc[:, D_LAT:] = rope[:n_pre]
    tok_acc[:, :D_LAT] = lat[n_pre:]
    tok_acc[:, D_LAT:] = rope[n_pre:]
    shares, chunk, _ = own_ref.shape
    tok = seq // heads
    spare = jnp.zeros((chunk - pre - tok, wide), f32)
    first_core = lax.rem(lax.axis_index("head"), 2) == 0
    for i in range(shares):
        pair = []
        for core in range(2):
            j = (HEAD_FIRST + 2 * i + core) % heads
            k = (2 * i + core) * pre
            piece = [pre_acc[k : k + pre], tok_acc[j * tok : (j + 1) * tok], spare]
            pair.append(jnp.concatenate(piece, axis=0))
        own_ref[i] = jnp.where(first_core, pair[0], pair[1]).astype(bf16)
        other_ref[i] = jnp.where(first_core, pair[1], pair[0]).astype(bf16)
    for copy in out:
        copy.wait()


def add_shares(own_ref, given_ref, out_ref):
    out_ref[...] = (own_ref[...].astype(f32) + given_ref[...].astype(f32)).astype(bf16)


def query_grads(key_ref, ds_ref, out_ref):
    out_ref[...] = dot_tn(key_ref[...], ds_ref[...]).astype(bf16)


def per_head(*shape):
    return pl.BlockSpec((None, *shape), lambda h: (h, 0, 0))


def keep(space, *arrays):
    return [pltpu.with_memory_space_constraint(x, space) for x in arrays]


def struct(shape, dtype):
    return jax.ShapeDtypeStruct(shape, dtype)


def cost(flops, nbytes, exps=0):
    return pl.CostEstimate(flops=int(flops), bytes_accessed=int(nbytes), transcendentals=int(exps))


def from_first(first, size):
    return [[(first + i) % size for i in range(size)]]


def shards(queries, d_out, tok_latent, w_uk, w_uv, pool, tenant_of_request, slot_of_tenant):
    heads = lax.axis_size("head")
    reqs = lax.axis_size("req")
    req_first = REQ_FIRST % reqs
    req_group = from_first(req_first, reqs)
    head_group = from_first(HEAD_FIRST % heads, heads)
    spread_group = from_first(SPREAD_FIRST % heads, heads)
    req_place = lax.axis_index("req")
    slot_ids = slot_of_tenant.at[tenant_of_request].get(mode="promise_in_bounds")
    my_slot = lax.dynamic_slice(slot_ids, (req_place,), (1,), allow_negative_indices=False)[0]
    lat = pool.shape[2]
    pre = pool.shape[1]
    seq, n_h, d_q = queries.shape
    d_v = d_out.shape[2]
    tok = seq // heads
    n_pre = pre * heads

    with jax.named_scope("fetch_slots"):
        mine = jnp.broadcast_to(pool, (reqs, pre, lat))
        all_slots = lax.all_to_all(mine, "req", 0, 0, axis_index_groups=req_group)

    q_t = jnp.transpose(queries, (1, 2, 0))
    with jax.named_scope("spread_prefix"):
        place = lax.rem(my_slot + (reqs - req_first), reqs)
        rows = lax.dynamic_slice(all_slots, (place, 0, 0), (1, pre, lat), allow_negative_indices=False).astype(bf16)
        rows, d_out = lax.optimization_barrier((rows, d_out))
        prefix = lax.all_to_all(jnp.broadcast_to(rows, (heads, pre, lat)), "head", 0, 0, axis_index_groups=spread_group)

    with jax.named_scope("project_tokens"):
        n_rows = max(x.stop for x in rows_held(n_h, seq).values())
        inputs = q_t.reshape(n_h * d_q, seq), d_out.reshape(seq, n_h * d_v), tok_latent.T, w_uk.reshape(n_h * D_NOPE, D_LAT), w_uv
        held = pl.pallas_call(
            project_tokens,
            in_specs=[ANYWHERE] * 5,
            out_specs=IN_VMEM,
            out_shape=pltpu.VMEM((n_rows, D_LAT), bf16),
            scratch_shapes=[
                pltpu.VMEM((lat, seq), bf16),
                pltpu.VMEM((n_h, D_LAT, d_v), bf16),
                pltpu.SemaphoreType.DMA((5,)),
            ],
            compiler_params=PARAMS,
            cost_estimate=cost(n_h * 1.0e8, 5e6),
        )(*keep(pltpu.HBM, *inputs))

    with jax.named_scope("key_grads"):
        own, other, d_scores, keys = pl.pallas_call(
            key_grads,
            in_specs=[IN_VMEM] * 2,
            out_specs=[IN_VMEM, IN_VMEM, ANYWHERE, ANYWHERE],
            out_shape=[
                pltpu.VMEM((heads // 2, CHUNK, lat), bf16),
                pltpu.VMEM((heads // 2, CHUNK, lat), bf16),
                pltpu.HBM((n_h, n_pre + seq, seq), bf16),
                pltpu.HBM((n_h, n_pre + seq, d_q), bf16),
            ],
            scratch_shapes=[
                pltpu.VMEM((n_h, n_pre + seq, seq), bf16),
                pltpu.VMEM((n_h, n_pre + seq, d_q), bf16),
                pltpu.VMEM((n_h, n_pre + seq, seq), bf16),
                pltpu.VMEM((n_pre, lat), f32),
                pltpu.VMEM((seq, lat), f32),
                pltpu.VMEM((n_pre, lat), f32),
                pltpu.SemaphoreType.DMA((n_h, 2)),
            ],
            compiler_params=PARAMS,
            cost_estimate=cost(n_h * 2.5e8, 5e6, n_h * seq * seq),
        )(prefix, *keep(pltpu.VMEM, held))

    with jax.named_scope("sum_heads"):
        given = lax.ppermute(other, "head", [(i, i ^ 1) for i in range(heads)])
        summed = pl.pallas_call(
            add_shares,
            in_specs=[IN_VMEM] * 2,
            out_specs=IN_VMEM,
            out_shape=pltpu.HBM(own.shape, bf16),
            compiler_params=PARAMS,
            cost_estimate=cost(2e5, 1e6),
        )(*keep(pltpu.VMEM, own), given)
        core_groups = [[i + core for i in head_group[0][::2]] for core in range(2)]
        parts = lax.all_to_all(summed, "head", 0, 0, axis_index_groups=core_groups)

    with jax.named_scope("query_grads"):
        d_q_t = pl.pallas_call(
            query_grads,
            grid=(n_h,),
            in_specs=[per_head(n_pre + seq, d_q), per_head(n_pre + seq, seq)],
            out_specs=per_head(d_q, seq),
            out_shape=struct((n_h, d_q, seq), bf16),
            compiler_params=PARAMS,
            cost_estimate=cost(n_h * 8e7, 3e6),
        )(*keep(pltpu.HBM, keys, d_scores))

    with jax.named_scope("sum_slots"):
        share = jnp.sum(parts.astype(f32), axis=0)
        token_grad = share[pre : pre + tok].astype(bf16)
        owned = jnp.roll(slot_ids, -req_first) == req_place
        sent, d_q_t, owned = lax.optimization_barrier((share[:pre].astype(bf16), d_q_t, owned))
        sent = jnp.broadcast_to(sent[None], (reqs, pre, lat))
        given = lax.all_to_all(sent, "req", 0, 0, axis_index_groups=req_group)
        pool_grad = jnp.sum(jnp.where(owned[:, None, None], given.astype(f32), 0.0), axis=0, keepdims=True)
    d_queries = jnp.transpose(d_q_t, (2, 0, 1))
    return d_queries, token_grad, pool_grad


def solution(mesh):
    return jax.shard_map(
        shards,
        mesh=mesh,
        in_specs=(
            P("req", "head", None),
            P("req", "head", None),
            P("req", None),
            P("head", None, None),
            P("head", None, None),
            P("req", "head", None),
            P(),
            P(),
        ),
        out_specs=(P("req", "head", None), P(("req", "head"), None), P("req", "head", None)),
        check_vma=False,
    )
```

```python
import jax
import jax.numpy as jnp
from jax import lax
from jax.experimental import pallas as pl
from jax.experimental.pallas import tpu as pltpu
from jax.sharding import PartitionSpec as P

D_LAT = 512
D_ROPE = 64
D_NOPE = 128
SCALE = float(D_NOPE + D_ROPE) ** (-0.5)
bf16 = jnp.bfloat16
f32 = jnp.float32
CHUNK = 16
BLOCK = 128
REQ_FIRST = 10
HEAD_FIRST = 20
SPREAD_FIRST = 20
ANYWHERE = pl.BlockSpec(memory_space=pl.ANY)
IN_VMEM = pl.BlockSpec(memory_space=pltpu.VMEM)
PARAMS = pltpu.CompilerParams(vmem_limit_bytes=24 * 1024 * 1024)


def dot(a, b):
    return jnp.dot(a, b, preferred_element_type=f32)


def dot_nt(a, b):
    return lax.dot_general(a, b, (((1,), (1,)), ((), ())), preferred_element_type=f32)


def dot_tn(a, b):
    return lax.dot_general(a, b, (((0,), (0,)), ((), ())), preferred_element_type=f32)


def project_tokens(qt_hbm, do_hbm, tokt_hbm, uk_hbm, uv_hbm, held_ref, tokt_ref, uv_ref, sems):
    n_h, _, d_v = uv_ref.shape
    seq = tokt_ref.shape[1]
    rows = rows_held(n_h, seq)
    copies = [
        pltpu.make_async_copy(tokt_hbm, tokt_ref, sems.at[0]),
        pltpu.make_async_copy(uk_hbm, held_ref.at[rows["uk"]], sems.at[1]),
        pltpu.make_async_copy(uv_hbm, uv_ref, sems.at[2]),
        pltpu.make_async_copy(do_hbm, held_ref.at[rows["do"]], sems.at[3]),
        pltpu.make_async_copy(qt_hbm, held_ref.at[rows["q"], :seq], sems.at[4]),
    ]
    for copy in copies:
        copy.start()
    copies[0].wait()
    tok = tokt_ref[...].T
    copies[1].wait()
    held_ref[rows["key"]] = dot_nt(tok[:, :D_LAT], held_ref[rows["uk"]]).astype(bf16)
    copies[2].wait()
    at = rows["uv"].start
    for h in range(n_h):
        mine = slice(h * d_v, (h + 1) * d_v)
        held_ref[at + h * d_v : at + (h + 1) * d_v] = uv_ref[h].T
        held_ref[rows["val"], mine] = dot(tok[:, :D_LAT], uv_ref[h]).astype(bf16)
    for copy in copies[3:]:
        copy.wait()
    at = rows["q"].start
    held_ref[at : at + seq, seq : seq + D_ROPE] = tok[:, D_LAT:]


def rows_held(n_h, seq):
    sizes = dict(uk=n_h * D_NOPE, uv=n_h * D_NOPE, do=seq, key=seq, val=seq, q=n_h * (D_NOPE + D_ROPE))
    places, at = {}, 0
    for name, size in sizes.items():
        places[name] = slice(at, at + size)
        at += size
    return places


def key_grads(
    parts_ref, held_ref,
    own_ref, other_ref, ds_hbm, key_hbm,
    ds_ref, key_ref, probs_ref, pre_f32, tok_acc, pre_acc, sems,
):
    n_h, n_keys, seq = ds_ref.shape
    heads, pre, wide = parts_ref.shape
    n_pre = n_keys - seq
    d_q = D_NOPE + D_ROPE
    rows = rows_held(n_h, seq)
    at_q = rows["q"].start
    row = lax.broadcasted_iota(jnp.int32, (BLOCK, BLOCK), 0)
    col = lax.broadcasted_iota(jnp.int32, (BLOCK, BLOCK), 1)
    for i in range(heads):
        pre_f32[i * pre : (i + 1) * pre] = parts_ref[i].astype(f32)
    prefix = pre_f32[...].astype(bf16)
    uk = held_ref[rows["uk"]]
    uv = held_ref[rows["uv"]]
    pre_keys = dot_nt(prefix[:, :D_LAT], uk).astype(bf16)
    pre_vals = dot_nt(prefix[:, :D_LAT], uv).astype(bf16)
    key_rope = jnp.concatenate([prefix[:, D_LAT:], held_ref[at_q : at_q + seq, seq : seq + D_ROPE]], axis=0)
    key_sides = []
    val_sides = []
    rope = None
    out = []
    for h in range(n_h):
        mine = slice(h * D_NOPE, (h + 1) * D_NOPE)
        q_rows = slice(at_q + h * d_q, at_q + (h + 1) * d_q)
        key_ref[h, :, :D_NOPE] = jnp.concatenate([pre_keys[:, mine], held_ref[rows["key"], mine]], axis=0)
        key_ref[h, :, D_NOPE:] = key_rope
        val = jnp.concatenate([pre_vals[:, mine], held_ref[rows["val"], mine]], axis=0)
        for at in range(0, seq, BLOCK):
            here = slice(at, at + BLOCK)
            seen = n_pre + at + BLOCK
            scores = dot(key_ref[h, :seen], held_ref[q_rows, here]) * SCALE
            edge = jnp.where(row <= col, scores[seen - BLOCK :], -1e30)
            scores = jnp.concatenate([scores[: seen - BLOCK], edge], axis=0)
            d_probs = dot_nt(val[:seen], held_ref[rows["do"], mine][here])
            terms = jnp.exp(scores - jnp.max(scores, axis=0, keepdims=True))
            probs = terms * (1.0 / jnp.sum(terms, axis=0, keepdims=True))
            delta = jnp.sum(probs * d_probs, axis=0, keepdims=True)
            probs_ref[h, :seen, here] = probs.astype(bf16)
            ds_ref[h, :seen, here] = (probs * (d_probs - delta)).astype(bf16)
            if seen < n_keys:
                probs_ref[h, seen:, here] = jnp.zeros((n_keys - seen, BLOCK), bf16)
                ds_ref[h, seen:, here] = jnp.zeros((n_keys - seen, BLOCK), bf16)
        for i, (kept, target) in enumerate(((key_ref, key_hbm), (ds_ref, ds_hbm))):
            out.append(pltpu.make_async_copy(kept.at[h], target.at[h], sems.at[h, i]))
            out[-1].start()
        ds_q = dot_nt(ds_ref[h], held_ref[q_rows, :seq]) * SCALE
        key_sides.append(ds_q[:, :D_NOPE].astype(bf16))
        val_sides.append(dot(probs_ref[h], held_ref[rows["do"], mine]).astype(bf16))
        rope = ds_q[:, D_NOPE:] if rope is None else rope + ds_q[:, D_NOPE:]
    lat = dot(jnp.concatenate(key_sides, axis=1), uk) + dot(jnp.concatenate(val_sides, axis=1), uv)
    pre_acc[:, :D_LAT] = lat[:n_pre]
    pre_acc[:, D_LAT:] = rope[:n_pre]
    tok_acc[:, :D_LAT] = lat[n_pre:]
    tok_acc[:, D_LAT:] = rope[n_pre:]
    shares, chunk, _ = own_ref.shape
    tok = seq // heads
    spare = jnp.zeros((chunk - pre - tok, wide), f32)
    first_core = lax.rem(lax.axis_index("head"), 2) == 0
    for i in range(shares):
        pair = []
        for core in range(2):
            j = (HEAD_FIRST + 2 * i + core) % heads
            k = (2 * i + core) * pre
            piece = [pre_acc[k : k + pre], tok_acc[j * tok : (j + 1) * tok], spare]
            pair.append(jnp.concatenate(piece, axis=0))
        own_ref[i] = jnp.where(first_core, pair[0], pair[1]).astype(bf16)
        other_ref[i] = jnp.where(first_core, pair[1], pair[0]).astype(bf16)
    for copy in out:
        copy.wait()


def add_shares(own_ref, given_ref, out_ref):
    out_ref[...] = (own_ref[...].astype(f32) + given_ref[...].astype(f32)).astype(bf16)


def query_grads(key_ref, ds_ref, out_ref):
    out_ref[...] = (dot_tn(key_ref[...], ds_ref[...]) * SCALE).astype(bf16)


def per_head(*shape):
    return pl.BlockSpec((None, *shape), lambda h: (h, 0, 0))


def keep(space, *arrays):
    return [pltpu.with_memory_space_constraint(x, space) for x in arrays]


def struct(shape, dtype):
    return jax.ShapeDtypeStruct(shape, dtype)


def cost(flops, nbytes, exps=0):
    return pl.CostEstimate(flops=int(flops), bytes_accessed=int(nbytes), transcendentals=int(exps))


def from_first(first, size):
    return [[(first + i) % size for i in range(size)]]


def shards(queries, d_out, tok_latent, w_uk, w_uv, pool, tenant_of_request, slot_of_tenant):
    heads = lax.axis_size("head")
    reqs = lax.axis_size("req")
    req_first = REQ_FIRST % reqs
    req_group = from_first(req_first, reqs)
    head_group = from_first(HEAD_FIRST % heads, heads)
    spread_group = from_first(SPREAD_FIRST % heads, heads)
    req_place = lax.axis_index("req")
    slot_ids = slot_of_tenant.at[tenant_of_request].get(mode="promise_in_bounds")
    my_slot = lax.dynamic_slice(slot_ids, (req_place,), (1,), allow_negative_indices=False)[0]
    lat = pool.shape[2]
    pre = pool.shape[1]
    seq, n_h, d_q = queries.shape
    d_v = d_out.shape[2]
    tok = seq // heads
    n_pre = pre * heads

    with jax.named_scope("fetch_slots"):
        mine = jnp.broadcast_to(pool, (reqs, pre, lat))
        all_slots = lax.all_to_all(mine, "req", 0, 0, axis_index_groups=req_group)

    q_t = jnp.transpose(queries, (1, 2, 0))
    with jax.named_scope("spread_prefix"):
        place = lax.rem(my_slot + (reqs - req_first), reqs)
        rows = lax.dynamic_slice(all_slots, (place, 0, 0), (1, pre, lat), allow_negative_indices=False).astype(bf16)
        rows, d_out = lax.optimization_barrier((rows, d_out))
        prefix = lax.all_to_all(jnp.broadcast_to(rows, (heads, pre, lat)), "head", 0, 0, axis_index_groups=spread_group)

    with jax.named_scope("project_tokens"):
        n_rows = max(x.stop for x in rows_held(n_h, seq).values())
        inputs = q_t.reshape(n_h * d_q, seq), d_out.reshape(seq, n_h * d_v), tok_latent.T, w_uk.reshape(n_h * D_NOPE, D_LAT), w_uv
        held = pl.pallas_call(
            project_tokens,
            in_specs=[ANYWHERE] * 5,
            out_specs=IN_VMEM,
            out_shape=pltpu.VMEM((n_rows, D_LAT), bf16),
            scratch_shapes=[
                pltpu.VMEM((lat, seq), bf16),
                pltpu.VMEM((n_h, D_LAT, d_v), bf16),
                pltpu.SemaphoreType.DMA((5,)),
            ],
            compiler_params=PARAMS,
            cost_estimate=cost(n_h * 1.0e8, 5e6),
        )(*keep(pltpu.HBM, *inputs))

    with jax.named_scope("key_grads"):
        own, other, d_scores, keys = pl.pallas_call(
            key_grads,
            in_specs=[IN_VMEM] * 2,
            out_specs=[IN_VMEM, IN_VMEM, ANYWHERE, ANYWHERE],
            out_shape=[
                pltpu.VMEM((heads // 2, CHUNK, lat), bf16),
                pltpu.VMEM((heads // 2, CHUNK, lat), bf16),
                pltpu.HBM((n_h, n_pre + seq, seq), bf16),
                pltpu.HBM((n_h, n_pre + seq, d_q), bf16),
            ],
            scratch_shapes=[
                pltpu.VMEM((n_h, n_pre + seq, seq), bf16),
                pltpu.VMEM((n_h, n_pre + seq, d_q), bf16),
                pltpu.VMEM((n_h, n_pre + seq, seq), bf16),
                pltpu.VMEM((n_pre, lat), f32),
                pltpu.VMEM((seq, lat), f32),
                pltpu.VMEM((n_pre, lat), f32),
                pltpu.SemaphoreType.DMA((n_h, 2)),
            ],
            compiler_params=PARAMS,
            cost_estimate=cost(n_h * 2.5e8, 5e6, n_h * seq * seq),
        )(prefix, *keep(pltpu.VMEM, held))

    with jax.named_scope("sum_heads"):
        given = lax.ppermute(other, "head", [(i, i ^ 1) for i in range(heads)])
        summed = pl.pallas_call(
            add_shares,
            in_specs=[IN_VMEM] * 2,
            out_specs=IN_VMEM,
            out_shape=pltpu.HBM(own.shape, bf16),
            compiler_params=PARAMS,
            cost_estimate=cost(2e5, 1e6),
        )(*keep(pltpu.VMEM, own), given)
        core_groups = [[i + core for i in head_group[0][::2]] for core in range(2)]
        parts = lax.all_to_all(summed, "head", 0, 0, axis_index_groups=core_groups)

    with jax.named_scope("query_grads"):
        d_q_t = pl.pallas_call(
            query_grads,
            grid=(n_h,),
            in_specs=[per_head(n_pre + seq, d_q), per_head(n_pre + seq, seq)],
            out_specs=per_head(d_q, seq),
            out_shape=struct((n_h, d_q, seq), bf16),
            compiler_params=PARAMS,
            cost_estimate=cost(n_h * 8e7, 3e6),
        )(*keep(pltpu.HBM, keys, d_scores))

    with jax.named_scope("sum_slots"):
        share = jnp.sum(parts.astype(f32), axis=0)
        token_grad = share[pre : pre + tok].astype(bf16)
        owned = jnp.roll(slot_ids, -req_first) == req_place
        sent, d_q_t, owned = lax.optimization_barrier((share[:pre].astype(bf16), d_q_t, owned))
        sent = jnp.broadcast_to(sent[None], (reqs, pre, lat))
        given = lax.all_to_all(sent, "req", 0, 0, axis_index_groups=req_group)
        pool_grad = jnp.sum(jnp.where(owned[:, None, None], given.astype(f32), 0.0), axis=0, keepdims=True)
    d_queries = jnp.transpose(d_q_t, (2, 0, 1))
    return d_queries, token_grad, pool_grad


def solution(mesh):
    return jax.shard_map(
        shards,
        mesh=mesh,
        in_specs=(
            P("req", "head", None),
            P("req", "head", None),
            P("req", None),
            P("head", None, None),
            P("head", None, None),
            P("req", "head", None),
            P(),
            P(),
        ),
        out_specs=(P("req", "head", None), P(("req", "head"), None), P("req", "head", None)),
        check_vma=False,
    )
```
